128 devices in a mesh: cache: 32 (over z, y, core), rank: 4 (over x).
Axes of the slice: x: 4, y: 4, z: 4, core: 2. Of those that a mesh axis runs over, the one named last changes fastest.
Arguments:
- hist_keys: bfloat16 [512, 640, 1024], P('cache', 'rank'), may hold values from -6 to 6
- hist_values: bfloat16 [512, 640, 1024], P('cache', 'rank'), may hold values from -6 to 6
- lengths: int32 [512], P('cache'), may hold values from 1 to 640, 163840 in all
- route: int32 [512, 1], P('cache'), may hold values from 0 to 31; in each aligned block of 16 rows (0 to 15, 16 to 31, ...) no two rows name the same one
- candidates: bfloat16 [32, 32, 128, 1024], P('cache', None, 'rank'), may hold values from -6 to 6
- w_qu: bfloat16 [1024, 2048], replicated, may hold values from -0.1875 to 0.1875
- w_out: bfloat16 [1024, 1024], replicated, may hold values from -0.1875 to 0.1875
Outputs:
- ranked: bfloat16 [32, 32, 128, 1024], P('cache', None, 'rank')
The draws below stay inside these ranges and needn't reach their ends.
Inputs may be any that keep to these rules, and one draw needn't show every extreme that they name: `route`: among the 16 users of one cache index no two name the same group.
All inputs are finite; a program needn't handle non-finite values. No bound on the sum of `lengths` on one device may be relied on, other than what follows from the above.
Results may differ from the reference program's by a relative error of at most 0.0033.
Values may be sent and summed in bfloat16 or wider, within the bound.
No kernel may reach another device: no remote copies, remote signals or barrier semaphores. Data moves between devices by JAX's collectives and lax.ppermute only.
A program may use at most 192 MiB of HBM per device.

```python
import math
import jax
import jax.numpy as jnp
import numpy as np
from jax import lax

D = 1024
HEADS = 8
HIST = 640
CAND = 128
GROUPS = 32
U_DEV = 16
USERS = 512


def block_scale(rng, extent, split, least, high):
    factor_of = 1.0
    for axis_at, shards_of in split:
        steps = jax.random.uniform(jax.random.fold_in(jax.random.fold_in(rng, 6), axis_at), (shards_of,), jnp.float32, least / len(split), high / len(split))
        factor_of = factor_of * jnp.repeat(jnp.exp(steps), extent[axis_at] // shards_of).reshape((-1,) + (1,) * (len(extent) - 1 - axis_at))
    return factor_of


def profile(amount, total, reach, lean):
    weights = [(1 << 20) // math.isqrt(grade ** lean) + 1 for grade in range(2, amount + 1)]
    surplus, given = total - reach - (amount - 1), [1] * (amount - 1)
    while surplus > 0:
        free = [i for i in range(amount - 1) if given[i] < reach]
        whole, budget = sum([weights[i] for i in free]), surplus
        for i in free:
            more = min(reach - given[i], max(1, budget * weights[i] // whole), surplus)
            given[i] = given[i] + more
            surplus = surplus - more
    return np.array([reach] + given)


def ragged(stream_key, number_of, total, reach, lean):
    if number_of == 2:
        one = jax.random.randint(stream_key, (), max(1, total - reach), min(reach, total - 1) + 1)
        return jnp.stack([one, total - one])
    tallies = jnp.asarray(profile(number_of, total, reach, lean), jnp.int32)
    twos = (number_of - 1) // 2
    giver, taker = tallies[1:1 + 2 * twos:2], tallies[2:2 + 2 * twos:2]
    slack = jnp.minimum(giver - 1, reach - taker)
    shifted = jax.random.randint(jax.random.fold_in(stream_key, 1), (twos,), 0, 1 << 20) % (slack + 1)
    tallies = tallies.at[1:1 + 2 * twos:2].set(giver - shifted).at[2:2 + 2 * twos:2].set(taker + shifted)
    return tallies[jax.random.permutation(jax.random.fold_in(stream_key, 2), number_of)]


def routed_block(rng, own, number, rows, count, top, bound, slope):
    sequence = jax.random.permutation(rng, count)
    crowded, ordinary = shares(count, rows * top, bound, slope, True), shares(count, rows * top, bound, slope, False)
    places = jnp.arange(count)

    def named(sizes, turn):
        used = int((sizes > 0).sum())
        fixed = max(1, used // 4)
        shifted = fixed + (places - fixed + turn * (used - fixed)) % max(1, count - fixed)
        return jnp.zeros((count,), jnp.int32).at[sequence[jnp.where(places < fixed, places, shifted)]].set(jnp.asarray(sizes, jnp.int32))

    sizes = jnp.where(number % 4 == 0, named(crowded, number // 4), named(ordinary, number - number // 4 - 1))
    mixed = jax.random.permutation(jax.random.fold_in(own, 3), count)
    donor, sink = mixed[0:count // 2 * 2:2], mixed[1:count // 2 * 2:2]
    slack = jnp.minimum(sizes[donor] - 1, bound - sizes[sink]) // 2
    slack = jnp.where((donor == sequence[0]) | (sink == sequence[0]) | (sizes[sink] == 0), 0, jnp.maximum(slack, 0))
    shifted = jax.random.randint(jax.random.fold_in(own, 4), (count // 2,), 0, 1 << 20) % (slack + 1)
    sizes = sizes.at[donor].add(-shifted).at[sink].add(shifted)
    labels = jnp.searchsorted(jnp.cumsum(sizes), jnp.arange(rows * top), side="right").astype(jnp.int32)
    listing = labels.reshape(top, rows).T
    listing = listing[jax.random.permutation(jax.random.fold_in(own, 1), rows)]
    turn = jax.random.randint(jax.random.fold_in(own, 2), (rows, 1), 0, top)
    return jnp.take_along_axis(listing, (jnp.arange(top)[None, :] + turn) % top, axis=1)


def shares(number_of, total, limit, skew, full):
    loads = [(1 << 20) // math.isqrt(rank ** skew) + 1 for rank in range(1, number_of + 1)]
    largest = limit if full else min(limit, max(-(-total // number_of), total * loads[0] // sum(loads)))
    least = 1 if total - largest >= number_of - 1 else 0
    counts, spare = [largest] + [least] * (number_of - 1), total - largest - least * (number_of - 1)
    while spare > 0:
        free = [i for i in range(1, number_of) if counts[i] < largest] or [i for i in range(1, number_of) if counts[i] < limit]
        whole, budget = sum([loads[i] for i in free]), spare
        for i in free:
            more = min(limit - counts[i], max(1, budget * loads[i] // whole), spare)
            counts[i] = counts[i] + more
            spare = spare - more
    return np.array(counts)


def normal_values(key, extent, scale, limit, cuts=(), kind=jnp.bfloat16):
    values = jax.random.normal(key, extent, jnp.float32) * scale
    if len(cuts) > 0:
        values = block_scale(key, extent, cuts, -0.22, 0.18) * values
    return jnp.clip(values, min=-limit, max=limit).astype(kind)


def setup_inputs(seed: int = 0) -> dict:
    streams_of = jax.random.split(jax.random.key(seed), 8)
    hist_keys = normal_values(streams_of[0], (USERS, HIST, D), 1.0, 6.0, ((0, 32), (1, 4)))
    hist_values = normal_values(streams_of[1], (USERS, HIST, D), 1.0, 6.0, ((0, 32), (1, 4)))
    lengths = ragged(streams_of[2], USERS, USERS * HIST // 2, HIST, 1).astype(jnp.int32)
    route_keys = jax.random.split(jax.random.fold_in(streams_of[3], 1), USERS // U_DEV)
    route_turns = jax.random.permutation(jax.random.fold_in(streams_of[3], 3), USERS // U_DEV)
    route = jax.vmap(lambda own, number: routed_block(jax.random.fold_in(streams_of[3], 2), own, number, U_DEV, GROUPS, 1, 1, 2))(route_keys, route_turns).reshape((USERS, 1))
    candidates = normal_values(streams_of[4], (GROUPS, GROUPS, CAND, D), 1.0, 6.0, ((0, 32), (2, 4)))
    w_qu = normal_values(streams_of[5], (D, 2 * D), D ** -0.5, 0.1875)
    w_out = normal_values(streams_of[6], (D, D), D ** -0.5, 0.1875)
    return dict(hist_keys=hist_keys, hist_values=hist_values, lengths=lengths, route=route, candidates=candidates, w_qu=w_qu, w_out=w_out)


EPS = 1e-05

def attend_block(query, keys, values):
    slots, cands, width = query.shape
    events = keys.shape[1]
    head_width = width // HEADS
    query_heads = query.reshape(slots, cands, HEADS, head_width).astype(jnp.float32)
    key_heads = keys.reshape(slots, events, HEADS, head_width).astype(jnp.float32)
    value_heads = values.reshape(slots, events, HEADS, head_width).astype(jnp.float32)
    scores = jnp.einsum('schd,srhd->shrc', query_heads, key_heads) * head_width ** (-0.5)
    weights = jax.nn.silu(scores).astype(jnp.bfloat16).astype(jnp.float32)
    mixed = jnp.einsum('shrc,srhd->schd', weights, value_heads)
    return mixed.reshape(slots, cands, width)

def reference(hist_keys, hist_values, lengths, route, candidates, w_qu, w_out):
    users = hist_keys.shape[0]
    groups = candidates.shape[0]
    owner_index = jnp.arange(users, dtype=jnp.int32) // U_DEV
    keep = (jnp.arange(HIST, dtype=jnp.int32)[None, :] < lengths[:, None])[:, :, None]
    zero = jnp.zeros((), jnp.bfloat16)
    keys_kept = jnp.where(keep, hist_keys, zero)
    values_kept = jnp.where(keep, hist_values, zero)
    slot_user = jnp.full((groups, groups), users, jnp.int32)
    slot_user = slot_user.at[route[:, 0], owner_index].set(jnp.arange(users, dtype=jnp.int32))

    def one_group(packed):
        features, index = packed
        valid = (index < users)[:, None, None]
        safe = jnp.minimum(index, users - 1)
        keys_here = jnp.where(valid, keys_kept[safe], zero)
        values_here = jnp.where(valid, values_kept[safe], zero)
        projected = jax.nn.silu(jnp.dot(features.reshape(-1, D), w_qu, preferred_element_type=jnp.float32))
        projected = projected.reshape(groups, CAND, 2 * D)
        queries = projected[:, :, :D].astype(jnp.bfloat16)
        gate = projected[:, :, D:].astype(jnp.bfloat16)
        mixed = attend_block(queries, keys_here, values_here)
        centred = mixed - lax.optimization_barrier(jnp.mean(mixed, axis=-1, keepdims=True))
        variance = lax.optimization_barrier(jnp.mean(centred * centred, axis=-1, keepdims=True))
        normed = centred * lax.rsqrt(variance + EPS)
        gated = (normed * gate.astype(jnp.float32)).astype(jnp.bfloat16)
        output = jnp.dot(gated.reshape(-1, D), w_out, preferred_element_type=jnp.float32).reshape(groups, CAND, D)
        return (features.astype(jnp.float32) + output).astype(jnp.bfloat16)
    return lax.map(one_group, (candidates, slot_user))
```

```python
import jax
import jax.numpy as jnp
from jax import lax
from jax.experimental import pallas as pl
from jax.experimental.pallas import tpu as pltpu
from jax.sharding import PartitionSpec as P

HEADS = 8
EPS = 1e-05
CHUNKS = 2
VMEM_LIMIT = 48 * 1024 * 1024

F32 = jnp.float32
BF16 = jnp.bfloat16


def whole():
    return pl.BlockSpec(memory_space=pltpu.VMEM)


def params(*semantics):
    return pltpu.CompilerParams(
        dimension_semantics=semantics or None, vmem_limit_bytes=VMEM_LIMIT
    )


def pick_kernel(route_ref, arrived_ref, picked_ref):
    for i in range(picked_ref.shape[0]):
        picked_ref[i] = arrived_ref[route_ref[i]]


def pick(route, arrived, users):
    _, cands, width = arrived.shape
    return pl.pallas_call(
        pick_kernel,
        grid_spec=pltpu.PrefetchScalarGridSpec(
            num_scalar_prefetch=1, grid=(), in_specs=[whole()], out_specs=whole()
        ),
        out_shape=jax.ShapeDtypeStruct((users, cands, width), BF16),
        compiler_params=params(),
        name="pick",
    )(route, arrived)


def attend_kernel(
    lengths_ref, rank_ref, own_ref, left_ref, right_ref, far_a_ref, far_b_ref, keys_ref, values_ref,
    out_own, out_left_a, out_left_b, out_right_a, out_right_b, out_far_a, out_far_b,
):
    step, half = pl.program_id(0), pl.num_programs(0)
    events, width = keys_ref.shape[2:]
    cands = own_ref.shape[2]
    head = 128
    factor = 0.5 * head ** (-0.5)
    for side, far_ref, out_left, out_right, out_far in (
        (0, far_a_ref, out_left_a, out_right_a, out_far_a),
        (1, far_b_ref, out_left_b, out_right_b, out_far_b),
    ):
        length = lengths_ref[step + side * half]
        position = rank_ref[0] * events + lax.broadcasted_iota(jnp.int32, (events, width), 0)
        keep = jnp.where(position < length, 1.0, 0.0).astype(BF16)
        queries = jnp.concatenate(
            [own_ref[side, 0], left_ref[side, 0], right_ref[side, 0], far_ref[0]], axis=0
        )
        keys = keys_ref[side, 0]
        values = values_ref[side, 0] * keep
        for h in range(width // head):
            cols = slice(h * head, (h + 1) * head)
            scores = lax.dot_general(
                queries[:, cols], keys[:, cols], (((1,), (1,)), ((), ())), preferred_element_type=F32
            )
            scaled = scores * factor
            weights = (scaled + scaled * jnp.tanh(scaled)).astype(BF16)
            mixed = jnp.dot(weights, values[:, cols], preferred_element_type=F32).astype(BF16)
            out_own[side, 0, :, cols] = mixed[:cands]
            out_left[0, :, cols] = mixed[cands:2 * cands]
            out_right[0, :, cols] = mixed[2 * cands:3 * cands]
            out_far[0, :, cols] = mixed[3 * cands:]


def attend(lengths, rank, own, left, right, far_a, far_b, keys, values, chunk):
    users, cands, width = own.shape
    half = users // 2
    events = keys.shape[1]

    def split(x):
        return x.reshape((2, half) + x.shape[1:])

    pair = pl.BlockSpec((2, 1, cands, width), lambda i, *_: (0, i, 0, 0))
    single = pl.BlockSpec((1, cands, width), lambda i, *_: (i, 0, 0))
    cached = pl.BlockSpec((2, 1, events, width), lambda i, *_: (0, i, 0, chunk))
    small = jax.ShapeDtypeStruct((half, cands, width), BF16)
    outs = pl.pallas_call(
        attend_kernel,
        grid_spec=pltpu.PrefetchScalarGridSpec(
            num_scalar_prefetch=2,
            grid=(half,),
            in_specs=[pair, pair, pair, single, single, cached, cached],
            out_specs=[pair] + [single] * 6,
        ),
        out_shape=[jax.ShapeDtypeStruct((2, half, cands, width), BF16)] + [small] * 6,
        compiler_params=params("arbitrary"),
        name="attend",
    )(lengths, rank, split(own), split(left), split(right), far_a, far_b, split(keys), split(values))
    return [outs[0].reshape(users, cands, width)] + list(outs[1:])


def place_kernel(route_ref, own_ref, left_a, left_b, right_a, right_b, placed_ref):
    users = own_ref.shape[0]
    half = users // 2
    placed_ref[...] = jnp.zeros_like(placed_ref)
    for i in range(users):
        left, right = (left_a, right_a) if i < half else (left_b, right_b)
        j = i % half
        total = own_ref[i].astype(F32) + left[j].astype(F32) + right[j].astype(F32)
        placed_ref[route_ref[i]] = total.astype(BF16)


def place(route, own, left_a, left_b, right_a, right_b, slots):
    _, cands, width = own.shape
    return pl.pallas_call(
        place_kernel,
        grid_spec=pltpu.PrefetchScalarGridSpec(
            num_scalar_prefetch=1, grid=(), in_specs=[whole()] * 5, out_specs=whole()
        ),
        out_shape=jax.ShapeDtypeStruct((slots, cands, width), BF16),
        compiler_params=params(),
        name="place",
    )(route, own, left_a, left_b, right_a, right_b)


def finish_kernel(*refs):
    mixed_refs, (gate_ref, features_ref, w_ref, out_ref) = refs[:-4], refs[-4:]
    mixed = jnp.concatenate([m[...] for m in mixed_refs], axis=1).astype(F32)
    centred = mixed - jnp.mean(mixed, axis=-1, keepdims=True)
    variance = jnp.mean(centred * centred, axis=-1, keepdims=True)
    normed = centred * lax.rsqrt(variance + EPS)
    gated = (normed * gate_ref[...].astype(F32)).astype(BF16)
    output = jnp.dot(gated, w_ref[...], preferred_element_type=F32)
    out_ref[...] = (features_ref[...].astype(F32) + output).astype(BF16)


def finish(mixed, gate, features, w_out, steps=4):
    rows, width = features.shape
    part = mixed[0].shape[1]
    block = rows // steps
    return pl.pallas_call(
        finish_kernel,
        grid=(steps,),
        in_specs=[pl.BlockSpec((block, part), lambda i: (i, 0))] * len(mixed)
        + [pl.BlockSpec((block, width), lambda i: (i, 0))] * 2
        + [pl.BlockSpec((width, width), lambda i: (0, 0))],
        out_specs=pl.BlockSpec((block, width), lambda i: (i, 0)),
        out_shape=jax.ShapeDtypeStruct((rows, width), BF16),
        compiler_params=params("arbitrary"),
        name="finish",
    )(*mixed, gate, features, w_out)


def rotate(x, by):
    n = 4
    return lax.ppermute(x, "rank", [(i, (i + by) % n) for i in range(n)])


def exchange(x):
    return lax.all_to_all(x, "cache", split_axis=0, concat_axis=0, tiled=True)


def per_device(hist_keys, hist_values, lengths, route, candidates, w_qu, w_out):
    users, hist_rows, width = hist_keys.shape
    slots, cands = candidates.shape[1:3]
    half = users // 2
    features = candidates.reshape(slots * cands, width)
    route = route[:, 0]
    rank = lax.axis_index("rank").astype(jnp.int32).reshape(1)
    part = width // CHUNKS

    def project(columns):
        return jax.nn.silu(jnp.dot(features, columns, preferred_element_type=F32)).astype(BF16)

    arrived = []
    for c in range(CHUNKS):
        queries = project(w_qu[:, c * part:(c + 1) * part])
        arrived.append(exchange(queries.reshape(slots, cands, part)))
    gate = project(w_qu[:, width:])
    mixed = []
    for c in range(CHUNKS):
        own = pick(route, arrived[c], users)
        left, right = rotate(own, 1), rotate(own, -1)
        far_a, far_b = rotate(left[:half], 1), rotate(right[half:], -1)
        p_own, p_left_a, p_left_b, p_right_a, p_right_b, p_far_a, p_far_b = attend(
            lengths, rank, own, left, right, far_a, far_b, hist_keys, hist_values, c
        )
        via_a, via_b = rotate(p_far_a, 1), rotate(p_far_b, -1)
        from_left_b, from_right_a = rotate(p_right_b, 1), rotate(p_left_a, -1)
        from_left_a = rotate((p_right_a.astype(F32) + via_a.astype(F32)).astype(BF16), 1)
        from_right_b = rotate((p_left_b.astype(F32) + via_b.astype(F32)).astype(BF16), -1)
        placed = place(route, p_own, from_left_a, from_left_b, from_right_a, from_right_b, slots)
        mixed.append(exchange(placed).reshape(slots * cands, part))
    ranked = finish(mixed, gate, features, w_out)
    return ranked.reshape(1, slots, cands, width)


def solution(mesh):
    placed = (
        P("cache", "rank", None),
        P("cache", "rank", None),
        P("cache"),
        P("cache", None),
        P("cache", None, "rank", None),
        P(),
        P(),
    )
    return jax.shard_map(
        per_device,
        mesh=mesh,
        in_specs=placed,
        out_specs=P("cache", None, "rank", None),
        check_vma=False,
    )
```

```python
import jax
import jax.numpy as jnp
from jax import lax
from jax.experimental import pallas as pl
from jax.experimental.pallas import tpu as pltpu
from jax.sharding import PartitionSpec as P

HEADS = 8
EPS = 1e-05
MIB = 1024 * 1024
CHUNKS = 2

F32 = jnp.float32
BF16 = jnp.bfloat16


def whole():
    return pl.BlockSpec(memory_space=pltpu.VMEM)


def params(mib):
    return pltpu.CompilerParams(vmem_limit_bytes=mib * MIB)


def pick_kernel(route_ref, arrived_ref, *picked_refs):
    half, _, part = picked_refs[0].shape
    for c in range(CHUNKS):
        cols = slice(c * part, (c + 1) * part)
        for side in range(2):
            for i in range(half):
                picked_refs[2 * c + side][i] = arrived_ref[route_ref[side * half + i], :, cols]


def pick(route, arrived, users):
    _, cands, width = arrived.shape
    half = jax.ShapeDtypeStruct((users // 2, cands, width // CHUNKS), BF16)
    outs = pl.pallas_call(
        pick_kernel,
        grid_spec=pltpu.PrefetchScalarGridSpec(
            num_scalar_prefetch=1, grid=(), in_specs=[whole()], out_specs=[whole()] * 2 * CHUNKS
        ),
        out_shape=[half] * 2 * CHUNKS,
        compiler_params=params(8),
        name="pick",
    )(route, arrived)
    return [outs[2 * c:2 * c + 2] for c in range(CHUNKS)]


def attend_kernel(lengths_ref, rank_ref, *refs):
    queries_refs, (keys_ref, values_ref), outs = refs[:8], refs[8:10], refs[10:]
    step = pl.program_id(0)
    half = lengths_ref.shape[0] // 2
    group, events, width = keys_ref.shape[1:]
    cands = outs[0].shape[1]
    head = 128
    factor = 0.5 * head ** (-0.5)
    position = rank_ref[0] * events + lax.broadcasted_iota(jnp.int32, (events, head), 0)
    jobs = [(side, u, h) for side in range(2) for u in range(group) for h in range(width // head)]
    keeps = {}
    for side in range(2):
        for u in range(group):
            length = lengths_ref[side * half + step * group + u]
            keeps[side, u] = jnp.where(position < length, 1.0, 0.0).astype(BF16)
    weights = []
    for side, u, h in jobs:
        cols = slice(h * head, (h + 1) * head)
        queries = jnp.concatenate([ref[u, :, cols] for ref in queries_refs[side::2]], axis=0)
        scores = lax.dot_general(
            queries,
            keys_ref[side, u, :, cols],
            (((1,), (1,)), ((), ())),
            preferred_element_type=F32,
        )
        scaled = scores * factor
        weights.append((scaled + scaled * jnp.tanh(scaled)).astype(BF16))
    for (side, u, h), weight in zip(jobs, weights):
        cols = slice(h * head, (h + 1) * head)
        values = values_ref[side, u, :, cols] * keeps[side, u]
        mixed = jnp.dot(weight, values, preferred_element_type=F32).astype(BF16)
        for n, out in enumerate(outs[side::2]):
            out[u, :, cols] = mixed[n * cands:(n + 1) * cands]


def attend(lengths, rank, queries, keys, values, chunk, group=2):
    half, cands, width = queries[0].shape
    events = keys.shape[1]

    def split(x):
        return x.reshape((2, half) + x.shape[1:])

    single = pl.BlockSpec((group, cands, width), lambda i, *_: (i, 0, 0))
    cached = pl.BlockSpec((2, group, events, width), lambda i, *_: (0, i, 0, chunk))
    return pl.pallas_call(
        attend_kernel,
        grid_spec=pltpu.PrefetchScalarGridSpec(
            num_scalar_prefetch=2,
            grid=(half // group,),
            in_specs=[single] * 8 + [cached] * 2,
            out_specs=[single] * 8,
        ),
        out_shape=[jax.ShapeDtypeStruct((half, cands, width), BF16)] * 8,
        compiler_params=params(48),
        name="attend",
    )(lengths, rank, *queries, split(keys), split(values))


def merge_kernel(right_ref, left_ref, via_a_ref, via_b_ref, to_right_ref, to_left_ref):
    to_right_ref[...] = (right_ref[...].astype(F32) + via_a_ref[...].astype(F32)).astype(BF16)
    to_left_ref[...] = (left_ref[...].astype(F32) + via_b_ref[...].astype(F32)).astype(BF16)


def merge(right_a, left_b, via_a, via_b):
    return pl.pallas_call(
        merge_kernel,
        in_specs=[whole()] * 4,
        out_specs=[whole()] * 2,
        out_shape=[jax.ShapeDtypeStruct(via_a.shape, BF16)] * 2,
        compiler_params=params(8),
        name="merge",
    )(right_a, left_b, via_a, via_b)


def place_kernel(route_ref, *refs):
    placed_ref = refs[-1]
    half, _, part = refs[0].shape
    width = part * CHUNKS
    placed_ref[...] = jnp.zeros_like(placed_ref)
    for side in range(2):
        for i in range(half):
            slot = route_ref[side * half + i]
            mixed = []
            for c in range(CHUNKS):
                own, left, right = (ref[i].astype(F32) for ref in refs[6 * c + side:6 * c + 6:2])
                mixed.append(own + left + right)
            mean = sum(jnp.sum(m, axis=-1, keepdims=True) for m in mixed) / width
            centred = [m - mean for m in mixed]
            variance = sum(jnp.sum(m * m, axis=-1, keepdims=True) for m in centred) / width
            scale = lax.rsqrt(variance + EPS)
            for c in range(CHUNKS):
                placed_ref[slot, :, c * part:(c + 1) * part] = (centred[c] * scale).astype(BF16)


def place(route, parts, slots):
    _, cands, part = parts[0].shape
    return pl.pallas_call(
        place_kernel,
        grid_spec=pltpu.PrefetchScalarGridSpec(
            num_scalar_prefetch=1, grid=(), in_specs=[whole()] * len(parts), out_specs=whole()
        ),
        out_shape=jax.ShapeDtypeStruct((slots, cands, part * CHUNKS), BF16),
        compiler_params=params(12),
        name="place",
    )(route, *parts)


def project_kernel(features_ref, w_ref, out_ref):
    projected = jnp.dot(features_ref[...], w_ref[...], preferred_element_type=F32)
    halved = 0.5 * projected
    out_ref[...] = (halved + halved * jnp.tanh(halved)).astype(BF16)


def project(features, w_qu, first, columns, steps=4):
    rows, width = features.shape
    block = rows // steps
    return pl.pallas_call(
        project_kernel,
        grid=(steps,),
        in_specs=[
            pl.BlockSpec((block, width), lambda i: (i, 0)),
            pl.BlockSpec((width, columns), lambda i: (0, first // columns)),
        ],
        out_specs=pl.BlockSpec((block, columns), lambda i: (i, 0)),
        out_shape=jax.ShapeDtypeStruct((rows, columns), BF16),
        compiler_params=params(62),
        name="project",
    )(features, w_qu)


def finish_kernel(normed_ref, gate_ref, features_ref, w_ref, out_ref):
    gated = (normed_ref[...].astype(F32) * gate_ref[...].astype(F32)).astype(BF16)
    output = jnp.dot(gated, w_ref[...], preferred_element_type=F32)
    out_ref[...] = (features_ref[...].astype(F32) + output).astype(BF16)


def finish(normed, gate, features, w_out, steps=4):
    rows, width = features.shape
    rows_spec = pl.BlockSpec((rows // steps, width), lambda i: (i, 0))
    return pl.pallas_call(
        finish_kernel,
        grid=(steps,),
        in_specs=[rows_spec] * 3 + [pl.BlockSpec((width, width), lambda i: (0, 0))],
        out_specs=rows_spec,
        out_shape=jax.ShapeDtypeStruct((rows, width), BF16),
        compiler_params=params(62),
        name="finish",
    )(normed, gate, features, w_out)


def rotate(x, by):
    n = 4
    return lax.ppermute(x, "rank", [(i, (i + by) % n) for i in range(n)])


def exchange(x):
    return lax.all_to_all(x, "cache", split_axis=0, concat_axis=0, tiled=True)


def after(x, *others):
    return lax.optimization_barrier((x,) + others)[0]


def per_device(hist_keys, hist_values, lengths, route, candidates, w_qu, w_out):
    users, _, width = hist_keys.shape
    slots, cands = candidates.shape[1:3]
    features = candidates.reshape(slots * cands, width)
    route = route[:, 0]
    rank = lax.axis_index("rank").astype(jnp.int32).reshape(1)

    queries = project(features, w_qu, 0, width)
    arrived = exchange(queries.reshape(slots, cands, width))
    gate = project(after(features, queries), w_qu, width, width)
    own = pick(route, arrived, users)
    gathered = []
    for c in range(CHUNKS):
        own_a, own_b = own[c]
        if c > 0:
            own_a, own_b = lax.optimization_barrier((own_a, own_b, *gathered[c - 1][2:6:3]))[:2]
        left_a, left_b = rotate(own_a, 1), rotate(own_b, 1)
        right_a, right_b = rotate(own_a, -1), rotate(own_b, -1)
        far_a, far_b = rotate(left_a, 1), rotate(right_b, -1)
        gathered.append([*own[c], left_a, left_b, right_a, right_b, far_a, far_b])
    parts = []
    for c in range(CHUNKS):
        p_own_a, p_own_b, p_left_a, p_left_b, p_right_a, p_right_b, p_far_a, p_far_b = attend(
            lengths, rank, gathered[c], hist_keys, hist_values, c
        )
        via_a, via_b = rotate(p_far_a, 1), rotate(p_far_b, -1)
        from_left_b, from_right_a = rotate(p_right_b, 1), rotate(p_left_a, -1)
        to_right_a, to_left_b = merge(p_right_a, p_left_b, via_a, via_b)
        from_left_a, from_right_b = rotate(to_right_a, 1), rotate(to_left_b, -1)
        parts += [p_own_a, p_own_b, from_left_a, from_left_b, from_right_a, from_right_b]
    normed = exchange(place(route, parts, slots)).reshape(slots * cands, width)
    ranked = finish(normed, gate, features, w_out)
    return ranked.reshape(1, slots, cands, width)


def solution(mesh):
    placed = (
        P("cache", "rank", None),
        P("cache", "rank", None),
        P("cache"),
        P("cache", None),
        P("cache", None, "rank", None),
        P(),
        P(),
    )
    return jax.shard_map(
        per_device,
        mesh=mesh,
        in_specs=placed,
        out_specs=P("cache", None, "rank", None),
        check_vma=False,
    )
```

```python
import jax
import jax.numpy as jnp
from jax import lax
from jax.experimental import pallas as pl
from jax.experimental.pallas import tpu as pltpu
from jax.sharding import PartitionSpec as P

HEADS = 8
EPS = 1e-05
MIB = 1024 * 1024
CHUNKS = 2

F32 = jnp.float32
BF16 = jnp.bfloat16


def whole():
    return pl.BlockSpec(memory_space=pltpu.VMEM)


def params(mib):
    return pltpu.CompilerParams(vmem_limit_bytes=mib * MIB)


def pick_kernel(route_ref, arrived_ref, *picked_refs):
    half = picked_refs[0].shape[0]
    for side in range(2):
        for i in range(half):
            picked_refs[side][i] = arrived_ref[route_ref[side * half + i]]


def pick(route, arrived, users):
    _, cands, width = arrived.shape
    half = jax.ShapeDtypeStruct((users // 2, cands, width), BF16)
    return pl.pallas_call(
        pick_kernel,
        grid_spec=pltpu.PrefetchScalarGridSpec(
            num_scalar_prefetch=1, grid=(), in_specs=[whole()], out_specs=[whole()] * 2
        ),
        out_shape=[half] * 2,
        compiler_params=params(8),
        name="pick",
    )(route, arrived)


def attend_kernel(lengths_ref, rank_ref, *refs):
    queries_refs, (keys_ref, values_ref) = refs[:8], refs[8:10]
    own_a, own_b, go_right, go_left, right_a, left_b = refs[10:]
    outs = (
        (own_a, go_left.at[1], right_a, go_right.at[0]),
        (own_b, left_b, go_right.at[1], go_left.at[0]),
    )
    step = pl.program_id(0)
    half = lengths_ref.shape[0] // 2
    group, events, width = keys_ref.shape[1:]
    cands = own_a.shape[1]
    head = 128
    factor = 0.5 * head ** (-0.5)
    position = rank_ref[0] * events + lax.broadcasted_iota(jnp.int32, (events, head), 0)
    jobs = [(side, u, h) for side in range(2) for u in range(group) for h in range(width // head)]
    keeps = {}
    for side in range(2):
        for u in range(group):
            length = lengths_ref[side * half + step * group + u]
            keeps[side, u] = jnp.where(position < length, 1.0, 0.0).astype(BF16)
    weights = []
    for side, u, h in jobs:
        cols = slice(h * head, (h + 1) * head)
        queries = jnp.concatenate([ref[u, :, cols] for ref in queries_refs[side::2]], axis=0)
        scores = lax.dot_general(
            queries,
            keys_ref[side, u, :, cols],
            (((1,), (1,)), ((), ())),
            preferred_element_type=F32,
        )
        scaled = scores * factor
        weights.append((scaled + scaled * jnp.tanh(scaled)).astype(BF16))
    for (side, u, h), weight in zip(jobs, weights):
        cols = slice(h * head, (h + 1) * head)
        values = values_ref[side, u, :, cols] * keeps[side, u]
        mixed = jnp.dot(weight, values, preferred_element_type=F32).astype(BF16)
        for n, out in enumerate(outs[side]):
            out[u, :, cols] = mixed[n * cands:(n + 1) * cands]


def attend(lengths, rank, queries, keys, values, chunk, group=2):
    half, cands, width = queries[0].shape
    events = keys.shape[1]

    def split(x):
        return x.reshape((2, half) + x.shape[1:])

    single = pl.BlockSpec((group, cands, width), lambda i, *_: (i, 0, 0))
    double = pl.BlockSpec((2, group, cands, width), lambda i, *_: (0, i, 0, 0))
    small = jax.ShapeDtypeStruct((half, cands, width), BF16)
    large = jax.ShapeDtypeStruct((2, half, cands, width), BF16)
    cached = pl.BlockSpec((2, group, events, width), lambda i, *_: (0, i, 0, chunk))
    return pl.pallas_call(
        attend_kernel,
        grid_spec=pltpu.PrefetchScalarGridSpec(
            num_scalar_prefetch=2,
            grid=(half // group,),
            in_specs=[single] * 8 + [cached] * 2,
            out_specs=[single] * 2 + [double] * 2 + [single] * 2,
        ),
        out_shape=[small] * 2 + [large] * 2 + [small] * 2,
        compiler_params=params(48),
        name="attend",
    )(lengths, rank, *queries, split(keys), split(values))


def merge_kernel(right_ref, left_ref, from_left_ref, from_right_ref, to_right_ref, to_left_ref):
    to_right_ref[...] = (right_ref[...].astype(F32) + from_left_ref[0].astype(F32)).astype(BF16)
    to_left_ref[...] = (left_ref[...].astype(F32) + from_right_ref[0].astype(F32)).astype(BF16)


def merge(right_a, left_b, from_left, from_right):
    return pl.pallas_call(
        merge_kernel,
        in_specs=[whole()] * 4,
        out_specs=[whole()] * 2,
        out_shape=[jax.ShapeDtypeStruct(right_a.shape, BF16)] * 2,
        compiler_params=params(8),
        name="merge",
    )(right_a, left_b, from_left, from_right)


def place_kernel(route_ref, *refs):
    placed_ref = refs[-1]
    half, _, part = refs[0].shape
    width = part * CHUNKS
    placed_ref[...] = jnp.zeros_like(placed_ref)
    for side in range(2):
        for i in range(half):
            slot = route_ref[side * half + i]
            mixed = []
            for c in range(CHUNKS):
                own_a, own_b, first_left, first_right, left_a, right_b = refs[6 * c:6 * c + 6]
                if side == 0:
                    own, left, right = own_a[i], left_a[i], first_right[1, i]
                else:
                    own, left, right = own_b[i], first_left[1, i], right_b[i]
                mixed.append(own.astype(F32) + left.astype(F32) + right.astype(F32))
            mean = sum(jnp.sum(m, axis=-1, keepdims=True) for m in mixed) / width
            centred = [m - mean for m in mixed]
            variance = sum(jnp.sum(m * m, axis=-1, keepdims=True) for m in centred) / width
            scale = lax.rsqrt(variance + EPS)
            for c in range(CHUNKS):
                placed_ref[slot, :, c * part:(c + 1) * part] = (centred[c] * scale).astype(BF16)


def place(route, parts, slots):
    _, cands, part = parts[0].shape
    return pl.pallas_call(
        place_kernel,
        grid_spec=pltpu.PrefetchScalarGridSpec(
            num_scalar_prefetch=1, grid=(), in_specs=[whole()] * len(parts), out_specs=whole()
        ),
        out_shape=jax.ShapeDtypeStruct((slots, cands, part * CHUNKS), BF16),
        compiler_params=params(12),
        name="place",
    )(route, *parts)


def project_kernel(features_ref, w_ref, out_ref):
    projected = jnp.dot(features_ref[...], w_ref[...], preferred_element_type=F32)
    halved = 0.5 * projected
    out_ref[...] = (halved + halved * jnp.tanh(halved)).astype(BF16)


def project(features, w_qu, first, columns, steps=4):
    rows, width = features.shape
    block = rows // steps
    return pl.pallas_call(
        project_kernel,
        grid=(steps,),
        in_specs=[
            pl.BlockSpec((block, width), lambda i: (i, 0)),
            pl.BlockSpec((width, columns), lambda i: (0, first // columns)),
        ],
        out_specs=pl.BlockSpec((block, columns), lambda i: (i, 0)),
        out_shape=jax.ShapeDtypeStruct((rows, columns), BF16),
        compiler_params=params(62),
        name="project",
    )(features, w_qu)


def finish_kernel(normed_ref, gate_ref, features_ref, w_ref, out_ref):
    gated = (normed_ref[...].astype(F32) * gate_ref[...].astype(F32)).astype(BF16)
    output = jnp.dot(gated, w_ref[...], preferred_element_type=F32)
    out_ref[...] = (features_ref[...].astype(F32) + output).astype(BF16)


def finish(normed, gate, features, w_out, steps=4):
    rows, width = features.shape
    rows_spec = pl.BlockSpec((rows // steps, width), lambda i: (i, 0))
    return pl.pallas_call(
        finish_kernel,
        grid=(steps,),
        in_specs=[rows_spec] * 3 + [pl.BlockSpec((width, width), lambda i: (0, 0))],
        out_specs=rows_spec,
        out_shape=jax.ShapeDtypeStruct((rows, width), BF16),
        compiler_params=params(62),
        name="finish",
    )(normed, gate, features, w_out)


def rotate(x, by):
    n = 4
    return lax.ppermute(x, "rank", [(i, (i + by) % n) for i in range(n)])


def exchange(x):
    return lax.all_to_all(x, "cache", split_axis=0, concat_axis=0, tiled=True)


def after(x, *others):
    return lax.optimization_barrier((x,) + others)[0]


def per_device(hist_keys, hist_values, lengths, route, candidates, w_qu, w_out):
    users, _, width = hist_keys.shape
    slots, cands = candidates.shape[1:3]
    features = candidates.reshape(slots * cands, width)
    route = route[:, 0]
    rank = lax.axis_index("rank").astype(jnp.int32).reshape(1)

    part = width // CHUNKS
    near, own, queries = [], [], []
    for c in range(CHUNKS):
        columns = w_qu[:, c * part:(c + 1) * part]
        projected = jax.nn.silu(jnp.dot(features, columns, preferred_element_type=F32)).astype(BF16)
        queries.append(projected.reshape(slots, cands, part))
    gate = project(after(features, *queries), w_qu, width, width)
    for c in range(CHUNKS):
        arrived = exchange(queries[c])
        own_a, own_b = pick(route, arrived, users)
        own.append((own_a, own_b))
        near.append([rotate(own_a, 1), rotate(own_b, 1), rotate(own_a, -1), rotate(own_b, -1)])
    parts = []
    for c in range(CHUNKS):
        left_a, left_b, right_a, right_b = near[c]
        if c > 0:
            left_a, right_b = lax.optimization_barrier((left_a, right_b, parts[0]))[:2]
        far_a, far_b = rotate(left_a, 1), rotate(right_b, -1)
        p_own_a, p_own_b, go_right, go_left, p_right_a, p_left_b = attend(
            lengths, rank, [*own[c], *near[c], far_a, far_b], hist_keys, hist_values, c
        )
        from_left, from_right = rotate(go_right, 1), rotate(go_left, -1)
        to_right, to_left = merge(p_right_a, p_left_b, from_left, from_right)
        parts += [p_own_a, p_own_b, from_left, from_right, rotate(to_right, 1), rotate(to_left, -1)]
    normed = exchange(place(route, parts, slots)).reshape(slots * cands, width)
    ranked = finish(normed, gate, features, w_out)
    return ranked.reshape(1, slots, cands, width)


def solution(mesh):
    placed = (
        P("cache", "rank", None),
        P("cache", "rank", None),
        P("cache"),
        P("cache", None),
        P("cache", None, "rank", None),
        P(),
        P(),
    )
    return jax.shard_map(
        per_device,
        mesh=mesh,
        in_specs=placed,
        out_specs=P("cache", None, "rank", None),
        check_vma=False,
    )
```

```python
import jax
import jax.numpy as jnp
from jax import lax
from jax.experimental import pallas as pl
from jax.experimental.pallas import tpu as pltpu
from jax.sharding import PartitionSpec as P

HEADS = 8
EPS = 1e-05
MIB = 1024 * 1024
CHUNKS = 2

F32 = jnp.float32
BF16 = jnp.bfloat16


def whole():
    return pl.BlockSpec(memory_space=pltpu.VMEM)


def params(mib):
    return pltpu.CompilerParams(vmem_limit_bytes=mib * MIB)


def pick_kernel(route_ref, arrived_ref, *picked_refs):
    half = picked_refs[0].shape[0]
    for side in range(2):
        for i in range(half):
            picked_refs[side][i] = arrived_ref[route_ref[side * half + i]]


def pick(route, arrived, users):
    _, cands, width = arrived.shape
    half = jax.ShapeDtypeStruct((users // 2, cands, width), BF16)
    return pl.pallas_call(
        pick_kernel,
        grid_spec=pltpu.PrefetchScalarGridSpec(
            num_scalar_prefetch=1, grid=(), in_specs=[whole()], out_specs=[whole()] * 2
        ),
        out_shape=[half] * 2,
        compiler_params=params(8),
        name="pick",
    )(route, arrived)


def attend_kernel(lengths_ref, rank_ref, *refs):
    queries_refs, (keys_ref, values_ref) = refs[:8], refs[8:10]
    own_a, own_b, go_right, go_left, right_a, left_b = refs[10:]
    outs = (
        (own_a, go_left.at[1], right_a, go_right.at[0]),
        (own_b, left_b, go_right.at[1], go_left.at[0]),
    )
    step = pl.program_id(0)
    half = lengths_ref.shape[0] // 2
    group, events, width = keys_ref.shape[1:]
    cands = own_a.shape[1]
    head = 128
    factor = 0.5 * head ** (-0.5)
    position = rank_ref[0] * events + lax.broadcasted_iota(jnp.int32, (events, head), 0)
    jobs = [(side, u, h) for side in range(2) for u in range(group) for h in range(width // head)]
    keeps = {}
    for side in range(2):
        for u in range(group):
            length = lengths_ref[side * half + step * group + u]
            keeps[side, u] = jnp.where(position < length, 1.0, 0.0).astype(BF16)
    weights = []
    for side, u, h in jobs:
        cols = slice(h * head, (h + 1) * head)
        queries = jnp.concatenate([ref[u, :, cols] for ref in queries_refs[side::2]], axis=0)
        scores = lax.dot_general(
            queries,
            keys_ref[side, u, :, cols],
            (((1,), (1,)), ((), ())),
            preferred_element_type=F32,
        )
        scaled = scores * factor
        weights.append((scaled + scaled * jnp.tanh(scaled)).astype(BF16))
    for (side, u, h), weight in zip(jobs, weights):
        cols = slice(h * head, (h + 1) * head)
        values = values_ref[side, u, :, cols] * keeps[side, u]
        mixed = jnp.dot(weight, values, preferred_element_type=F32).astype(BF16)
        for n, out in enumerate(outs[side]):
            out[u, :, cols] = mixed[n * cands:(n + 1) * cands]


def attend(lengths, rank, queries, keys, values, chunk, group=4):
    half, cands, width = queries[0].shape
    events = keys.shape[1]

    def split(x):
        return x.reshape((2, half) + x.shape[1:])

    single = pl.BlockSpec((group, cands, width), lambda i, *_: (i, 0, 0))
    double = pl.BlockSpec((2, group, cands, width), lambda i, *_: (0, i, 0, 0))
    small = jax.ShapeDtypeStruct((half, cands, width), BF16)
    large = jax.ShapeDtypeStruct((2, half, cands, width), BF16)
    cached = pl.BlockSpec((2, group, events, width), lambda i, *_: (0, i, 0, chunk))
    return pl.pallas_call(
        attend_kernel,
        grid_spec=pltpu.PrefetchScalarGridSpec(
            num_scalar_prefetch=2,
            grid=(half // group,),
            in_specs=[single] * 8 + [cached] * 2,
            out_specs=[single] * 2 + [double] * 2 + [single] * 2,
        ),
        out_shape=[small] * 2 + [large] * 2 + [small] * 2,
        compiler_params=params(48),
        name="attend",
    )(lengths, rank, *queries, split(keys), split(values))


def merge_kernel(right_ref, left_ref, from_left_ref, from_right_ref, to_right_ref, to_left_ref):
    to_right_ref[...] = (right_ref[...].astype(F32) + from_left_ref[0].astype(F32)).astype(BF16)
    to_left_ref[...] = (left_ref[...].astype(F32) + from_right_ref[0].astype(F32)).astype(BF16)


def merge(right_a, left_b, from_left, from_right):
    return pl.pallas_call(
        merge_kernel,
        in_specs=[whole()] * 4,
        out_specs=[whole()] * 2,
        out_shape=[jax.ShapeDtypeStruct(right_a.shape, BF16)] * 2,
        compiler_params=params(8),
        name="merge",
    )(right_a, left_b, from_left, from_right)


def place_kernel(route_ref, *refs):
    placed_ref = refs[-1]
    half, _, part = refs[0].shape
    width = part * CHUNKS
    placed_ref[...] = jnp.zeros_like(placed_ref)
    for side in range(2):
        for i in range(half):
            slot = route_ref[side * half + i]
            mixed = []
            for c in range(CHUNKS):
                own_a, own_b, first_left, first_right, left_a, right_b = refs[6 * c:6 * c + 6]
                if side == 0:
                    own, left, right = own_a[i], left_a[i], first_right[1, i]
                else:
                    own, left, right = own_b[i], first_left[1, i], right_b[i]
                mixed.append(own.astype(F32) + left.astype(F32) + right.astype(F32))
            mean = sum(jnp.sum(m, axis=-1, keepdims=True) for m in mixed) / width
            centred = [m - mean for m in mixed]
            variance = sum(jnp.sum(m * m, axis=-1, keepdims=True) for m in centred) / width
            scale = lax.rsqrt(variance + EPS)
            for c in range(CHUNKS):
                placed_ref[slot, :, c * part:(c + 1) * part] = (centred[c] * scale).astype(BF16)


def place(route, parts, slots):
    _, cands, part = parts[0].shape
    return pl.pallas_call(
        place_kernel,
        grid_spec=pltpu.PrefetchScalarGridSpec(
            num_scalar_prefetch=1, grid=(), in_specs=[whole()] * len(parts), out_specs=whole()
        ),
        out_shape=jax.ShapeDtypeStruct((slots, cands, part * CHUNKS), BF16),
        compiler_params=params(12),
        name="place",
    )(route, *parts)


def project_kernel(features_ref, w_ref, out_ref):
    projected = jnp.dot(features_ref[...], w_ref[...], preferred_element_type=F32)
    halved = 0.5 * projected
    out_ref[...] = (halved + halved * jnp.tanh(halved)).astype(BF16)


def project(features, w_qu, first, columns, steps=4):
    rows, width = features.shape
    block = rows // steps
    return pl.pallas_call(
        project_kernel,
        grid=(steps,),
        in_specs=[
            pl.BlockSpec((block, width), lambda i: (i, 0)),
            pl.BlockSpec((width, columns), lambda i: (0, first // columns)),
        ],
        out_specs=pl.BlockSpec((block, columns), lambda i: (i, 0)),
        out_shape=jax.ShapeDtypeStruct((rows, columns), BF16),
        compiler_params=params(62),
        name="project",
    )(features, w_qu)


def finish_kernel(normed_ref, gate_ref, features_ref, w_ref, out_ref):
    gated = (normed_ref[...].astype(F32) * gate_ref[...].astype(F32)).astype(BF16)
    output = jnp.dot(gated, w_ref[...], preferred_element_type=F32)
    out_ref[...] = (features_ref[...].astype(F32) + output).astype(BF16)


def finish(normed, gate, features, w_out, steps=4):
    rows, width = features.shape
    rows_spec = pl.BlockSpec((rows // steps, width), lambda i: (i, 0))
    return pl.pallas_call(
        finish_kernel,
        grid=(steps,),
        in_specs=[rows_spec] * 3 + [pl.BlockSpec((width, width), lambda i: (0, 0))],
        out_specs=rows_spec,
        out_shape=jax.ShapeDtypeStruct((rows, width), BF16),
        compiler_params=params(62),
        name="finish",
    )(normed, gate, features, w_out)


def rotate(x, by):
    n = 4
    return lax.ppermute(x, "rank", [(i, (i + by) % n) for i in range(n)])


def exchange(x):
    return lax.all_to_all(x, "cache", split_axis=0, concat_axis=0, tiled=True)


def after(x, *others):
    return lax.optimization_barrier((x,) + others)[0]


def per_device(hist_keys, hist_values, lengths, route, candidates, w_qu, w_out):
    users, _, width = hist_keys.shape
    slots, cands = candidates.shape[1:3]
    features = candidates.reshape(slots * cands, width)
    route = route[:, 0]
    rank = lax.axis_index("rank").astype(jnp.int32).reshape(1)

    part = width // CHUNKS
    near, own, queries = [], [], []
    for c in range(CHUNKS):
        columns = w_qu[:, c * part:(c + 1) * part]
        projected = jax.nn.silu(jnp.dot(features, columns, preferred_element_type=F32)).astype(BF16)
        queries.append(projected.reshape(slots, cands, part))
    gate = project(after(features, *queries), w_qu, width, width)
    for c in range(CHUNKS):
        arrived = exchange(queries[c])
        own_a, own_b = pick(route, arrived, users)
        own.append((own_a, own_b))
        near.append([rotate(own_a, 1), rotate(own_b, 1), rotate(own_a, -1), rotate(own_b, -1)])
    parts = []
    for c in range(CHUNKS):
        left_a, left_b, right_a, right_b = near[c]
        if c > 0:
            left_a, right_b = lax.optimization_barrier((left_a, right_b, parts[0]))[:2]
        far_a, far_b = rotate(left_a, 1), rotate(right_b, -1)
        p_own_a, p_own_b, go_right, go_left, p_right_a, p_left_b = attend(
            lengths, rank, [*own[c], *near[c], far_a, far_b], hist_keys, hist_values, c
        )
        from_left, from_right = rotate(go_right, 1), rotate(go_left, -1)
        to_right, to_left = merge(p_right_a, p_left_b, from_left, from_right)
        parts += [p_own_a, p_own_b, from_left, from_right, rotate(to_right, 1), rotate(to_left, -1)]
    normed = exchange(place(route, parts, slots)).reshape(slots * cands, width)
    ranked = finish(normed, gate, features, w_out)
    return ranked.reshape(1, slots, cands, width)


def solution(mesh):
    placed = (
        P("cache", "rank", None),
        P("cache", "rank", None),
        P("cache"),
        P("cache", None),
        P("cache", None, "rank", None),
        P(),
        P(),
    )
    return jax.shard_map(
        per_device,
        mesh=mesh,
        in_specs=placed,
        out_specs=P("cache", None, "rank", None),
        check_vma=False,
    )
```
